256 devices in a mesh: patch: 32 (over x, y, z_hi), head: 8 (over z_lo, core).
Axes of the slice: x: 4, y: 4, z: 8 (z_hi: 2, z_lo: 4; z = z_hi * 4 + z_lo), core: 2. Of those that a mesh axis runs over, the one named last changes fastest.
Arguments:
- hidden: bfloat16 [2, 6144, 3072], P(None, 'patch', 'head'), may hold values from -6 to 6
- stale_kv: bfloat16 [2, 6144, 3072], P(None, 'patch', 'head'), may hold values from -8 to 8
- modulation: float32 [2, 2, 3072], replicated, may hold values from -3 to 3
- attn_gate: float32 [2, 3072], P(None, 'head'), may hold values from 0.5 to 2
- w_qkv: bfloat16 [3072, 3, 3072], P(None, None, 'head'), may hold values from -2 to 2
- w_out: bfloat16 [3072, 3072], P('head'), may hold values from -0.109375 to 0.109375
Outputs:
- updated: bfloat16 [2, 6144, 3072], P(None, 'patch', 'head')
The draws below stay inside these ranges and needn't reach their ends.
All inputs are finite; a program needn't handle non-finite values.
Results may differ from the reference program's by a relative error of at most 0.019.
Values may be sent and summed in bfloat16 or wider, within the bound.
No kernel may reach another device: no remote copies, remote signals or barrier semaphores. Data moves between devices by JAX's collectives and lax.ppermute only.
A program may use at most 128 MiB of HBM per device.

```python
import jax
import jax.numpy as jnp
from jax import lax

D = 3072
HEADS = 24
HEAD_DIM = 128
TOK_DEV = 192
STEPS = 2
TOKENS = 6144
N_PATCH = 32


def draw_hidden(key, part):
    key = jax.random.fold_in(key, 11)
    drawn = jax.random.normal(key, (STEPS, TOKENS, D), jnp.float32)
    return jnp.clip(drawn, -6.0, 6.0).astype(jnp.bfloat16)


def draw_modulation(key, part):
    key = jax.random.fold_in(key, 37)
    drawn = 0.5 * jax.random.normal(key, (STEPS, 2, D), jnp.float32)
    return jnp.clip(drawn, -3.0, 3.0).astype(jnp.float32)


def draw_w_qkv(key, part):
    key = jax.random.fold_in(key, 23)
    inverse_root = D ** (-0.5)
    normal_part = jnp.clip(jax.random.normal(key, (D, 3, D), jnp.float32), -6.0, 6.0)
    column_scale = jnp.array([1.6, 1.6, 1.0], jnp.float32) * inverse_root
    drawn = normal_part * column_scale[None, :, None]
    return jnp.clip(drawn, -2.0, 2.0).astype(jnp.bfloat16)


def level_of(key, extent, cuts, low, largest):
    loudness, own = 1.0, jax.random.fold_in(key, 6)
    for dim, shards_of in cuts:
        heights = jnp.exp(jax.random.uniform(jax.random.fold_in(own, dim), (shards_of,), jnp.float32, low / len(cuts), largest / len(cuts)))
        loudness = loudness * jnp.repeat(heights, extent[dim] // shards_of).reshape([-1 if axis == dim else 1 for axis in range(len(extent))])
    return loudness


def scatter_about(own_key, dims, width, most, pieces=(), kind=jnp.bfloat16):
    loudness = level_of(own_key, dims, pieces, -0.22, 0.18) if pieces else 1.0
    entries = jax.random.normal(own_key, dims, jnp.float32) * width * loudness
    return jnp.minimum(jnp.maximum(entries, -most), most).astype(kind)


def setup_inputs(seed: int = 0) -> dict:
    key_of = jax.random.split(jax.random.key(seed), 7)
    return {
        "hidden": draw_hidden(jax.random.fold_in(key_of[6], 71), 0),
        "stale_kv": scatter_about(key_of[1], (2, TOKENS, D), 1.5, 8.0, ((1, 32), (2, 8))),
        "modulation": draw_modulation(jax.random.fold_in(key_of[6], 71), 0),
        "attn_gate": jnp.clip(0.5 + 1.5 * jax.random.uniform(key_of[3], (STEPS, D), jnp.float32) ** level_of(key_of[3], (STEPS, D), ((1, 8),), -0.2, 0.2), 0.5, 2.0),
        "w_qkv": draw_w_qkv(jax.random.fold_in(key_of[6], 71), 0),
        "w_out": scatter_about(key_of[5], (D, D), D ** -0.5, 0.109375, ((0, 8),)),
    }


def layer_norm(values_in):
    mean_value = lax.optimization_barrier(jnp.mean(values_in, axis=-1, keepdims=True))
    centred = values_in - mean_value
    variance = lax.optimization_barrier(jnp.mean(centred * centred, axis=-1, keepdims=True))
    return centred * lax.rsqrt(variance + 1e-06)

def attend(queries, key_rows, value_rows):
    query_float = queries.astype(jnp.float32).reshape(TOK_DEV, HEADS, HEAD_DIM)
    key_float = key_rows.astype(jnp.float32).reshape(TOKENS, HEADS, HEAD_DIM)
    value_float = value_rows.astype(jnp.float32).reshape(TOKENS, HEADS, HEAD_DIM)
    scores = jnp.einsum('qhd,khd->qhk', query_float, key_float) * HEAD_DIM ** (-0.5)
    row_peak = lax.optimization_barrier(jnp.max(scores, axis=-1, keepdims=True))
    weights = lax.optimization_barrier(jnp.exp(scores - row_peak).astype(jnp.bfloat16))
    weights_float = weights.astype(jnp.float32)
    row_total = lax.optimization_barrier(jnp.sum(weights_float, axis=-1))
    weighted = jnp.einsum('qhk,khd->qhd', weights_float, value_float)
    return (weighted / row_total[..., None]).astype(jnp.bfloat16).reshape(TOK_DEV, D)

def reference(hidden, stale_kv, modulation, attn_gate, w_qkv, w_out):
    previous_keys = stale_kv[0]
    previous_values = stale_kv[1]
    results = []
    for step_index in range(STEPS):
        normed = layer_norm(hidden[step_index].astype(jnp.float32))
        normed = (normed * (1.0 + modulation[step_index, 1]) + modulation[step_index, 0]).astype(jnp.bfloat16)
        queries = jnp.dot(normed, w_qkv[:, 0, :], preferred_element_type=jnp.float32).astype(jnp.bfloat16)
        fresh_keys = jnp.dot(normed, w_qkv[:, 1, :], preferred_element_type=jnp.float32).astype(jnp.bfloat16)
        fresh_values = jnp.dot(normed, w_qkv[:, 2, :], preferred_element_type=jnp.float32).astype(jnp.bfloat16)

        def one_slab(slab_index, queries=queries, fresh_keys=fresh_keys, fresh_values=fresh_values, previous_keys=previous_keys, previous_values=previous_values):
            offset_row = (slab_index * TOK_DEV).astype(jnp.int32)
            zero_col = jnp.int32(0)
            own_keys = lax.dynamic_slice(fresh_keys, (offset_row, zero_col), (TOK_DEV, D))
            own_values = lax.dynamic_slice(fresh_values, (offset_row, zero_col), (TOK_DEV, D))
            key_rows = lax.dynamic_update_slice(previous_keys, own_keys, (offset_row, zero_col))
            value_rows = lax.dynamic_update_slice(previous_values, own_values, (offset_row, zero_col))
            slab_queries = lax.dynamic_slice(queries, (offset_row, zero_col), (TOK_DEV, D))
            return attend(slab_queries, key_rows, value_rows)
        attended = lax.map(one_slab, jnp.arange(N_PATCH, dtype=jnp.int32)).reshape(TOKENS, D)
        branch = jnp.dot(attended, w_out, preferred_element_type=jnp.float32)
        results.append((hidden[step_index].astype(jnp.float32) + attn_gate[step_index] * branch).astype(jnp.bfloat16))
        previous_keys = fresh_keys
        previous_values = fresh_values
    return jnp.stack(results)
```

```python
import functools

import jax
import jax.numpy as jnp
from jax import lax
from jax.experimental import pallas as pl
from jax.experimental.pallas import tpu as pltpu
from jax.sharding import Mesh
from jax.sharding import PartitionSpec as P

HEAD_DIM = 128
STEPS = 2
NX, NY, NZH, NZL, NC = 4, 4, 2, 4, 2
AXES = ("x", "y", "zh", "zl", "c")
EXP2_SCALE = HEAD_DIM**-0.5 * 1.4426950408889634
F32 = jnp.float32
BF16 = jnp.bfloat16
VMEM = pl.BlockSpec(memory_space=pltpu.VMEM)
SMEM = pl.BlockSpec(memory_space=pltpu.SMEM)
HBM = pl.BlockSpec(memory_space=pl.ANY)


def device_index(x, y, zh, zl, c):
    return (((x % NX) * NY + y % NY) * NZH + zh % NZH) * NZL * NC + (zl % NZL) * NC + c % NC


def permute(array, move):
    pairs = []
    for x in range(NX):
        for y in range(NY):
            for zh in range(NZH):
                for zl in range(NZL):
                    for c in range(NC):
                        target = move(x, y, zh, zl, c)
                        pairs.append((device_index(x, y, zh, zl, c), device_index(*target)))
    return lax.ppermute(array, AXES, pairs)


def along_keys(array, k):
    return permute(array, lambda x, y, zh, zl, c: (x, y + k, zh, zl, c) if c else (x + k, y, zh, zl, c))


def along_queries(array, k):
    return permute(array, lambda x, y, zh, zl, c: (x + k, y, zh, zl, c) if c else (x, y + k, zh, zl, c))


def other_half(array):
    return permute(array, lambda x, y, zh, zl, c: (x, y, zh + 1, zl, c))


def other_core(array):
    return permute(array, lambda x, y, zh, zl, c: (x, y, zh, zl, c + 1))


def along_heads(array, k):
    return permute(array, lambda x, y, zh, zl, c: (x, y, zh, zl + k, c))


def project_kernel(order, *refs):
    pieces = refs[:8]
    mod, w, q_out, kv_out, wbuf, normed, sems = refs[8:]
    width = pieces[0].shape[1]
    copies = []
    for i in range(8):
        rows = pl.ds(pl.multiple_of(order[i] * width, width), width)
        copy = pltpu.make_async_copy(
            w.at[:, rows, :], wbuf.at[:, pl.ds(i * width, width), :], sems.at[i]
        )
        copy.start()
        copies.append(copy)
    total = sum(jnp.sum(p[...].astype(F32), axis=-1, keepdims=True) for p in pieces)
    mean = total / (8.0 * width)
    square = sum(
        jnp.sum(jnp.square(p[...].astype(F32) - mean), axis=-1, keepdims=True) for p in pieces
    )
    inverse = lax.rsqrt(square / (8.0 * width) + 1e-06)
    for i in range(8):
        shift_scale = mod[order[i]]
        value = (pieces[i][...].astype(F32) - mean) * inverse
        value = value * (1.0 + shift_scale[1:2]) + shift_scale[0:1]
        normed[:, i * width : (i + 1) * width] = value.astype(BF16)
    for copy in copies:
        copy.wait()
    for j in range(3):
        result = jnp.dot(normed[...], wbuf[j], preferred_element_type=F32).astype(BF16)
        if j == 0:
            q_out[...] = result
        else:
            kv_out[j - 1] = result


def project(order, pieces, mod, w):
    rows, width = pieces[0].shape
    return pl.pallas_call(
        project_kernel,
        out_shape=(
            jax.ShapeDtypeStruct((rows, width), BF16),
            jax.ShapeDtypeStruct((2, rows, width), BF16),
        ),
        in_specs=[SMEM] + [VMEM] * 9 + [HBM],
        out_specs=(VMEM, VMEM),
        scratch_shapes=[
            pltpu.VMEM((3, 8 * width, width), BF16),
            pltpu.VMEM((rows, 8 * width), BF16),
            pltpu.SemaphoreType.DMA((8,)),
        ],
        compiler_params=pltpu.CompilerParams(vmem_limit_bytes=40 * 2**20),
        cost_estimate=pl.CostEstimate(
            flops=2 * rows * 24 * width * width, bytes_accessed=2 * 24 * width * width, transcendentals=0
        ),
        name="project",
    )(order, *pieces, mod, w)


def split3(value):
    first = value.astype(BF16)
    rest = value - first.astype(F32)
    second = rest.astype(BF16)
    third = (rest - second.astype(F32)).astype(BF16)
    return first, second, third


def attend_kernel(*refs):
    queries, fresh, held, outs = refs[:4], refs[4], refs[5:13], refs[13:]
    rows = queries[0].shape[0]
    lane = lax.broadcasted_iota(jnp.int32, (rows, HEAD_DIM), 1)
    marks = [jnp.zeros((rows, HEAD_DIM), F32) for _ in range(4)]
    ones = jnp.ones((8 * rows, HEAD_DIM), BF16)
    for h in range(3):
        cols = slice(h * HEAD_DIM, (h + 1) * HEAD_DIM)
        common_keys = [held[j][0, :, cols] for j in range(1, 8)]
        common_values = [held[j][1, :, cols] for j in range(1, 8)]
        for i in range(4):
            own = fresh if i == 0 else held[0]
            keys = jnp.concatenate([own[0, :, cols]] + common_keys, axis=0)
            values = jnp.concatenate([own[1, :, cols]] + common_values, axis=0)
            values = jnp.concatenate([values, ones], axis=1)
            scores = lax.dot_general(
                queries[i][:, cols], keys, (((1,), (1,)), ((), ())), preferred_element_type=F32
            )
            peak = jnp.max(scores, axis=-1, keepdims=True)
            weights = jnp.exp2((scores - peak) * EXP2_SCALE).astype(BF16)
            summed = jnp.dot(weights, values, preferred_element_type=F32)
            outs[i][:, cols] = summed[:, :HEAD_DIM].astype(BF16)
            parts = split3(peak) + split3(summed[:, HEAD_DIM : HEAD_DIM + 1])
            for n, part in enumerate(parts):
                marks[i] = jnp.where(lane == 6 * h + n, part.astype(F32), marks[i])
    for i in range(4):
        outs[i][:, 3 * HEAD_DIM :] = marks[i].astype(BF16)


def attend(queries, fresh, held):
    rows, width = queries[0].shape
    shape = jax.ShapeDtypeStruct((rows, width + HEAD_DIM), BF16)
    return pl.pallas_call(
        attend_kernel,
        out_shape=(shape,) * 4,
        in_specs=[VMEM] * 13,
        out_specs=(VMEM,) * 4,
        compiler_params=pltpu.CompilerParams(vmem_limit_bytes=40 * 2**20),
        cost_estimate=pl.CostEstimate(
            flops=4 * 4 * rows * 8 * rows * width,
            bytes_accessed=20 * 2 * rows * width,
            transcendentals=4 * rows * 8 * rows * 3,
        ),
        name="attend",
    )(*queries, fresh, *held)


def output_kernel(order, p0, p1, p2, p3, w, keep, send):
    parts = (p0, p1, p2, p3)
    width = keep.shape[2]
    marks = [p[:, 3 * HEAD_DIM :].astype(F32) for p in parts]
    attended = []
    for h in range(3):
        cols = slice(h * HEAD_DIM, (h + 1) * HEAD_DIM)

        def read(mark, first):
            return mark[:, first : first + 1] + mark[:, first + 1 : first + 2] + mark[:, first + 2 : first + 3]

        peaks = [read(mark, 6 * h) for mark in marks]
        sums = [read(mark, 6 * h + 3) for mark in marks]
        peak = functools.reduce(jnp.maximum, peaks)
        factors = [jnp.exp2((one - peak) * EXP2_SCALE) for one in peaks]
        total = sum(f * s for f, s in zip(factors, sums))
        weighted = sum(f * p[:, cols].astype(F32) for f, p in zip(factors, parts))
        attended.append((weighted / total).astype(BF16))
    attended = jnp.concatenate(attended, axis=1)
    for n in range(4):
        for side, out in enumerate((keep, send)):
            cols = pl.ds(pl.multiple_of(order[2 * n + side] * width, width), width)
            out[n] = jnp.dot(attended, w[:, cols], preferred_element_type=F32).astype(BF16)


def project_out(order, partials, w_out):
    rows = partials[0].shape[0]
    width = w_out.shape[0]
    shape = jax.ShapeDtypeStruct((4, rows, width), BF16)
    return pl.pallas_call(
        output_kernel,
        out_shape=(shape, shape),
        in_specs=[SMEM] + [VMEM] * 5,
        out_specs=(VMEM, VMEM),
        compiler_params=pltpu.CompilerParams(vmem_limit_bytes=40 * 2**20),
        cost_estimate=pl.CostEstimate(
            flops=2 * rows * 8 * width * width, bytes_accessed=16 * width * width, transcendentals=0
        ),
        name="project_out",
    )(order, *partials, w_out)


def on_device(hidden, stale_kv, modulation, attn_gate, w_qkv, w_out):
    width = hidden.shape[2]
    zl, core = lax.axis_index("zl"), lax.axis_index("c")
    order = jnp.stack(
        [((zl + n) % NZL) * NC + (core + s) % NC for n in range(4) for s in range(2)]
    ).astype(jnp.int32)
    w = jnp.transpose(w_qkv, (1, 0, 2))
    mods = jnp.transpose(modulation.reshape(STEPS, 2, 8, width), (0, 2, 1, 3))

    def gather_hidden(rows):
        pieces = [rows] + [along_heads(rows, -n) for n in (1, 2, 3)]
        return [p for piece in pieces for p in (piece, other_core(piece))]

    def gather_keys(pair):
        near = [pair] + [along_keys(pair, k) for k in (1, -1, 2)]
        opposite = other_half(pair)
        return near + [opposite] + [along_keys(opposite, k) for k in (1, -1, 2)]

    projected = []
    for s in range(STEPS):
        projected.append(project(order, gather_hidden(hidden[s]), mods[s], w))
    previous = stale_kv
    results = []
    for s in range(STEPS):
        queries, fresh = projected[s]
        moved = [queries] + [along_queries(queries, k) for k in (1, -1, 2)]
        partials = attend(moved, fresh, gather_keys(previous))
        partials = [partials[0]] + [along_queries(p, -k) for p, k in zip(partials[1:], (1, -1, 2))]
        keep, send = project_out(order, partials, w_out)
        pair_sum = keep.astype(F32) + other_core(send).astype(F32)
        branch = pair_sum[0]
        for n in (1, 2, 3):
            branch = branch + along_heads(pair_sum[n].astype(BF16), n).astype(F32)
        results.append((hidden[s].astype(F32) + attn_gate[s] * branch).astype(BF16))
        previous = fresh
    return jnp.stack(results)


def solution(mesh):
    fine = Mesh(mesh.devices.reshape(NX, NY, NZH, NZL, NC), AXES)
    patch, head = ("x", "y", "zh"), ("zl", "c")
    in_specs = (
        P(None, patch, head),
        P(None, patch, head),
        P(),
        P(None, head),
        P(None, None, head),
        P(head, None),
    )
    return jax.shard_map(
        on_device, mesh=fine, in_specs=in_specs, out_specs=P(None, patch, head), check_vma=False
    )
```

```python
import functools

import jax
import jax.numpy as jnp
from jax import lax
from jax.experimental import pallas as pl
from jax.experimental.pallas import tpu as pltpu
from jax.sharding import Mesh
from jax.sharding import PartitionSpec as P

HEAD_DIM = 128
STEPS = 2
NX, NY, NZH, NZL, NC = 4, 4, 2, 4, 2
AXES = ("x", "y", "zh", "zl", "c")
EXP2_SCALE = HEAD_DIM**-0.5 * 1.4426950408889634
F32 = jnp.float32
BF16 = jnp.bfloat16
VMEM = pl.BlockSpec(memory_space=pltpu.VMEM)
SMEM = pl.BlockSpec(memory_space=pltpu.SMEM)
HBM = pl.BlockSpec(memory_space=pl.ANY)


def device_index(x, y, zh, zl, c):
    return (((x % NX) * NY + y % NY) * NZH + zh % NZH) * NZL * NC + (zl % NZL) * NC + c % NC


def permute(array, move):
    pairs = []
    for x in range(NX):
        for y in range(NY):
            for zh in range(NZH):
                for zl in range(NZL):
                    for c in range(NC):
                        target = move(x, y, zh, zl, c)
                        pairs.append((device_index(x, y, zh, zl, c), device_index(*target)))
    return lax.ppermute(array, AXES, pairs)


def along_keys(array, k):
    return permute(array, lambda x, y, zh, zl, c: (x, y + k, zh, zl, c) if c else (x + k, y, zh, zl, c))


def along_queries(array, k):
    return permute(array, lambda x, y, zh, zl, c: (x + k, y, zh, zl, c) if c else (x, y + k, zh, zl, c))


def other_half(array):
    return permute(array, lambda x, y, zh, zl, c: (x, y, zh + 1, zl, c))


def other_core(array):
    return permute(array, lambda x, y, zh, zl, c: (x, y, zh, zl, c + 1))


def along_heads(array, k):
    return permute(array, lambda x, y, zh, zl, c: (x, y, zh, zl + k, c))


def project_kernel(step, order, hidden, swapped, *refs):
    pieces = [hidden.at[step], swapped.at[step]] + list(refs[:6])
    mod, w, q_in, q_out, kv_out, normed = refs[6:]
    width = hidden.shape[2]
    total = sum(jnp.sum(p[...].astype(F32), axis=-1, keepdims=True) for p in pieces)
    mean = total / (8.0 * width)
    square = sum(
        jnp.sum(jnp.square(p[...].astype(F32) - mean), axis=-1, keepdims=True) for p in pieces
    )
    inverse = lax.rsqrt(square / (8.0 * width) + 1e-06)
    for i in range(8):
        shift_scale = mod[order[i]]
        value = (pieces[i][...].astype(F32) - mean) * inverse
        value = value * (1.0 + shift_scale[1:2]) + shift_scale[0:1]
        normed[:, pl.ds(pl.multiple_of(order[i] * width, width), width)] = value.astype(BF16)
    for j in range(3):
        result = jnp.dot(normed[...], w[j], preferred_element_type=F32).astype(BF16)
        if j:
            kv_out[j - 1] = result
        elif step == 0:
            q_out[...] = result
        else:
            q_out[0] = q_in[...]
            q_out[1] = result


def project(step, order, hidden, swapped, pieces, mod, w, q_in):
    _, rows, width = hidden.shape
    q_shape = (2, rows, width) if step else (rows, width)
    return pl.pallas_call(
        functools.partial(project_kernel, step),
        out_shape=(
            jax.ShapeDtypeStruct(q_shape, BF16),
            jax.ShapeDtypeStruct((2, rows, width), BF16),
        ),
        in_specs=[SMEM] + [VMEM] * 11,
        out_specs=(VMEM, VMEM),
        scratch_shapes=[pltpu.VMEM((rows, 8 * width), BF16)],
        compiler_params=pltpu.CompilerParams(vmem_limit_bytes=40 * 2**20),
        cost_estimate=pl.CostEstimate(
            flops=2 * rows * 24 * width * width, bytes_accessed=2 * 24 * width * width, transcendentals=0
        ),
        name="project",
    )(order, hidden, swapped, *pieces, mod, w, q_in)


def split3(value):
    first = value.astype(BF16)
    rest = value - first.astype(F32)
    second = rest.astype(BF16)
    third = (rest - second.astype(F32)).astype(BF16)
    return first, second, third


def attend_kernel(step, *refs):
    queries, fresh, held, outs = refs[:4], refs[4], refs[5:13], refs[13:]
    queries = [q.at[step] for q in queries]
    rows = queries[0].shape[0]
    lane = lax.broadcasted_iota(jnp.int32, (rows, HEAD_DIM), 1)
    marks = [jnp.zeros((rows, HEAD_DIM), F32) for _ in range(4)]
    ones = jnp.ones((8 * rows, HEAD_DIM), BF16)
    for h in range(3):
        cols = slice(h * HEAD_DIM, (h + 1) * HEAD_DIM)
        common_keys = [held[j][0, :, cols] for j in range(1, 8)]
        common_values = [held[j][1, :, cols] for j in range(1, 8)]
        for i in range(4):
            own = fresh if i == 0 else held[0]
            keys = jnp.concatenate([own[0, :, cols]] + common_keys, axis=0)
            values = jnp.concatenate([own[1, :, cols]] + common_values, axis=0)
            values = jnp.concatenate([values, ones], axis=1)
            scores = lax.dot_general(
                queries[i][:, cols], keys, (((1,), (1,)), ((), ())), preferred_element_type=F32
            )
            peak = jnp.max(scores, axis=-1, keepdims=True)
            weights = jnp.exp2((scores - peak) * EXP2_SCALE).astype(BF16)
            summed = jnp.dot(weights, values, preferred_element_type=F32)
            outs[i][:, cols] = summed[:, :HEAD_DIM].astype(BF16)
            parts = split3(peak) + split3(summed[:, HEAD_DIM : HEAD_DIM + 1])
            for n, part in enumerate(parts):
                marks[i] = jnp.where(lane == 6 * h + n, part.astype(F32), marks[i])
    for i in range(4):
        outs[i][:, 3 * HEAD_DIM :] = marks[i].astype(BF16)


def attend(step, queries, fresh, held):
    _, rows, width = queries[0].shape
    shape = jax.ShapeDtypeStruct((rows, width + HEAD_DIM), BF16)
    return pl.pallas_call(
        functools.partial(attend_kernel, step),
        out_shape=(shape,) * 4,
        in_specs=[VMEM] * 13,
        out_specs=(VMEM,) * 4,
        compiler_params=pltpu.CompilerParams(vmem_limit_bytes=40 * 2**20),
        cost_estimate=pl.CostEstimate(
            flops=4 * 4 * rows * 8 * rows * width,
            bytes_accessed=20 * 2 * rows * width,
            transcendentals=4 * rows * 8 * rows * 3,
        ),
        name="attend",
    )(*queries, fresh, *held)


def output_kernel(order, p0, p1, p2, p3, w, keep, send):
    parts = (p0, p1, p2, p3)
    width = keep.shape[2]
    marks = [p[:, 3 * HEAD_DIM :].astype(F32) for p in parts]
    attended = []
    for h in range(3):
        cols = slice(h * HEAD_DIM, (h + 1) * HEAD_DIM)

        def read(mark, first):
            return mark[:, first : first + 1] + mark[:, first + 1 : first + 2] + mark[:, first + 2 : first + 3]

        peaks = [read(mark, 6 * h) for mark in marks]
        sums = [read(mark, 6 * h + 3) for mark in marks]
        peak = functools.reduce(jnp.maximum, peaks)
        factors = [jnp.exp2((one - peak) * EXP2_SCALE) for one in peaks]
        total = sum(f * s for f, s in zip(factors, sums))
        weighted = sum(f * p[:, cols].astype(F32) for f, p in zip(factors, parts))
        attended.append((weighted / total).astype(BF16))
    attended = jnp.concatenate(attended, axis=1)
    for n in range(4):
        for side, out in enumerate((keep, send)):
            cols = pl.ds(pl.multiple_of(order[2 * n + side] * width, width), width)
            out[n] = jnp.dot(attended, w[:, cols], preferred_element_type=F32).astype(BF16)


def project_out(order, partials, w_out):
    rows = partials[0].shape[0]
    width = w_out.shape[0]
    shape = jax.ShapeDtypeStruct((4, rows, width), BF16)
    return pl.pallas_call(
        output_kernel,
        out_shape=(shape, shape),
        in_specs=[SMEM] + [VMEM] * 5,
        out_specs=(VMEM, VMEM),
        compiler_params=pltpu.CompilerParams(vmem_limit_bytes=40 * 2**20),
        cost_estimate=pl.CostEstimate(
            flops=2 * rows * 8 * width * width, bytes_accessed=16 * width * width, transcendentals=0
        ),
        name="project_out",
    )(order, *partials, w_out)


def on_device(hidden, stale_kv, modulation, attn_gate, w_qkv, w_out):
    width = hidden.shape[2]
    zl, core = lax.axis_index("zl"), lax.axis_index("c")
    order = jnp.stack(
        [((zl + n) % NZL) * NC + (core + s) % NC for n in range(4) for s in range(2)]
    ).astype(jnp.int32)
    w = jnp.transpose(w_qkv, (1, 0, 2))
    mods = jnp.transpose(modulation.reshape(STEPS, 2, 8, width), (0, 2, 1, 3))

    def after(array, *earlier):
        return lax.optimization_barrier((array, *earlier))[0]

    steps = [hidden[0], hidden[1]]
    ring = [[along_heads(rows, -1)] for rows in steps]
    swapped = other_core(hidden)
    stale = [stale_kv, along_keys(stale_kv, 1), along_keys(stale_kv, -1)]
    stale.append(along_keys(after(stale_kv, swapped), 2))
    crossed = [[], []]
    for hop in range(3):
        for s in range(STEPS):
            if hop < 2:
                ring[s].append(along_heads(ring[s][hop], -1))
            crossed[s].append(other_core(ring[s][hop]))
    opposite = other_half(after(stale_kv, ring[1][1]))

    def pieces_of(s):
        return [p for n in range(3) for p in (ring[s][n], crossed[s][n])]

    q_first, fresh_first = project(0, order, hidden, swapped, pieces_of(0), mods[0], w, steps[0])
    fresh_opposite = other_half(fresh_first)
    fresh_near = [fresh_first] + [along_keys(fresh_first, k) for k in (1, -1, 2)]
    queries, fresh_last = project(1, order, hidden, swapped, pieces_of(1), mods[1], w, q_first)
    moved = [queries] + [along_queries(queries, k) for k in (1, -1, 2)]
    stale_far = [opposite] + [along_keys(opposite, k) for k in (1, -1, 2)]
    fresh_far = [fresh_opposite] + [along_keys(fresh_opposite, k) for k in (1, -1, 2)]
    results = []
    for s in range(STEPS):
        if s == 0:
            partials = attend(s, moved, fresh_first, stale + stale_far)
        else:
            partials = attend(s, moved, fresh_last, fresh_near + fresh_far)
        partials = [partials[0]] + [along_queries(p, -k) for p, k in zip(partials[1:], (1, -1, 2))]
        keep, send = project_out(order, partials, w_out)
        pair_sum = keep.astype(F32) + other_core(send).astype(F32)
        branch = pair_sum[0]
        for n in (1, 2, 3):
            branch = branch + along_heads(pair_sum[n].astype(BF16), n).astype(F32)
        results.append((hidden[s].astype(F32) + attn_gate[s] * branch).astype(BF16))
    return jnp.stack(results)


def solution(mesh):
    fine = Mesh(mesh.devices.reshape(NX, NY, NZH, NZL, NC), AXES)
    patch, head = ("x", "y", "zh"), ("zl", "c")
    in_specs = (
        P(None, patch, head),
        P(None, patch, head),
        P(),
        P(None, head),
        P(None, None, head),
        P(head, None),
    )
    return jax.shard_map(
        on_device, mesh=fine, in_specs=in_specs, out_specs=P(None, patch, head), check_vma=False
    )
```

```python
import functools

import jax
import jax.numpy as jnp
from jax import lax
from jax.experimental import pallas as pl
from jax.experimental.pallas import tpu as pltpu
from jax.sharding import Mesh
from jax.sharding import PartitionSpec as P

HEAD_DIM = 128
STEPS = 2
NX, NY, NZH, NZL, NC = 4, 4, 2, 4, 2
AXES = ("x", "y", "zh", "zl", "c")
EXP2_SCALE = HEAD_DIM**-0.5 * 1.4426950408889634
F32 = jnp.float32
BF16 = jnp.bfloat16
VMEM = pl.BlockSpec(memory_space=pltpu.VMEM)
SMEM = pl.BlockSpec(memory_space=pltpu.SMEM)
HBM = pl.BlockSpec(memory_space=pltpu.HBM)
LIGHT = pl.CostEstimate(flops=1024, bytes_accessed=1024, transcendentals=0)


def device_index(x, y, zh, zl, c):
    return (((x % NX) * NY + y % NY) * NZH + zh % NZH) * NZL * NC + (zl % NZL) * NC + c % NC


def permute(array, move):
    pairs = []
    for x in range(NX):
        for y in range(NY):
            for zh in range(NZH):
                for zl in range(NZL):
                    for c in range(NC):
                        target = move(x, y, zh, zl, c)
                        pairs.append((device_index(x, y, zh, zl, c), device_index(*target)))
    return lax.ppermute(array, AXES, pairs)


def along_keys(array, k):
    return permute(array, lambda x, y, zh, zl, c: (x, y + k, zh, zl, c) if c else (x + k, y, zh, zl, c))


def along_queries(array, k):
    return permute(array, lambda x, y, zh, zl, c: (x + k, y, zh, zl, c) if c else (x, y + k, zh, zl, c))


def other_half(array):
    return permute(array, lambda x, y, zh, zl, c: (x, y, zh + 1, zl, c))


def other_core(array):
    return permute(array, lambda x, y, zh, zl, c: (x, y, zh, zl, c + 1))


def along_heads(array, k):
    return permute(array, lambda x, y, zh, zl, c: (x, y, zh, zl + k, c))


def call(body, outs, operands, hbm=(), smem=(), scratch=(), megabytes=24):
    specs = [HBM if i in hbm else SMEM if i in smem else VMEM for i in range(len(operands))]
    return pl.pallas_call(
        body,
        out_shape=[jax.ShapeDtypeStruct(shape, dtype) for shape, dtype in outs],
        in_specs=specs,
        out_specs=[VMEM] * len(outs),
        scratch_shapes=scratch,
        compiler_params=pltpu.CompilerParams(vmem_limit_bytes=megabytes * 2**20),
        cost_estimate=LIGHT,
    )(*operands)


def pass_kernel(rows, *refs):
    copy = pltpu.make_async_copy(rows, refs[-2], refs[-1])
    copy.start()
    copy.wait()


def pass_after(rows, *earlier):
    scratch = [pltpu.SemaphoreType.DMA]
    return call(pass_kernel, [(rows.shape, rows.dtype)], (rows, *earlier), hbm=(0,), scratch=scratch)[0]


def collect_kernel(own, first, second, third, *refs):
    out, sem = refs[-2:]
    copy = pltpu.make_async_copy(own, out.at[0], sem)
    copy.start()
    for n, piece in enumerate((first, second, third)):
        out[n + 1] = piece[...]
    copy.wait()


def normalize(step, order, pieces, mod, normed):
    pieces = [p.at[n, step] for n in range(4) for p in pieces]
    width = pieces[0].shape[1]
    total = sum(jnp.sum(p[...].astype(F32), axis=-1, keepdims=True) for p in pieces)
    mean = total / (8.0 * width)
    square = sum(
        jnp.sum(jnp.square(p[...].astype(F32) - mean), axis=-1, keepdims=True) for p in pieces
    )
    inverse = lax.rsqrt(square / (8.0 * width) + 1e-06)
    for i in range(8):
        shift_scale = mod[step, :, pl.ds(pl.multiple_of(order[i] * width, width), width)]
        value = (pieces[i][...].astype(F32) - mean) * inverse
        value = value * (1.0 + shift_scale[1:2]) + shift_scale[0:1]
        normed[:, pl.ds(pl.multiple_of(order[i] * width, width), width)] = value.astype(BF16)


def load(operands, buffers, sems):
    copies = [
        pltpu.make_async_copy(far, near, sems.at[n])
        for n, (far, near) in enumerate(zip(operands, buffers))
    ]
    for copy in copies:
        copy.start()
    return copies


def project_kernel(order, own, swapped, mod, w, *refs):
    queries, first, last, normed, mod_near, w_near, sems = refs[-7:]
    parts = [(mod, mod_near)] + [(w.at[j], w_near.at[j]) for j in (1, 2, 0)]
    copies = load(*zip(*parts), sems)
    copies[0].wait()
    for step in range(STEPS):
        normalize(step, order, (own, swapped), mod_near, normed)
        for n, j in enumerate((1, 2, 0)):
            if step == 0:
                copies[n + 1].wait()
            result = jnp.dot(normed[...], w_near[j], preferred_element_type=F32).astype(BF16)
            if j == 0:
                queries[step] = result
            else:
                (first, last)[step][j - 1] = result


def project(order, own, swapped, modulation, w, *others):
    _, _, rows, width = own.shape
    pair = ((2, rows, width), BF16)
    return call(
        project_kernel,
        [pair] * 3,
        (order, own, swapped, modulation, w, *others),
        hbm=(3, 4),
        smem=(0,),
        scratch=[
            pltpu.VMEM((rows, 8 * width), BF16),
            pltpu.VMEM(modulation.shape, F32),
            pltpu.VMEM(w.shape, BF16),
            pltpu.SemaphoreType.DMA((4,)),
        ],
        megabytes=50,
    )


def sum_kernel(keep, received, *refs):
    refs[-4][...] = keep[0].astype(F32) + received[0].astype(F32)
    for n, out in enumerate(refs[-3:]):
        out[...] = (keep[n + 1].astype(F32) + received[n + 1].astype(F32)).astype(BF16)


def split3(value):
    first = value.astype(BF16)
    rest = value - first.astype(F32)
    second = rest.astype(BF16)
    third = (rest - second.astype(F32)).astype(BF16)
    return first, second, third


def attend_kernel(step, *refs):
    queries, fresh, held, outs = refs[:4], refs[4], refs[5:13], refs[-4:]
    queries = [q.at[step] for q in queries]
    rows = queries[0].shape[0]
    lane = lax.broadcasted_iota(jnp.int32, (rows, HEAD_DIM), 1)
    marks = [jnp.zeros((rows, HEAD_DIM), F32) for _ in range(4)]
    ones = jnp.ones((8 * rows, HEAD_DIM), BF16)
    for h in range(3):
        cols = slice(h * HEAD_DIM, (h + 1) * HEAD_DIM)
        common_keys = [held[j][0, :, cols] for j in range(1, 8)]
        common_values = [held[j][1, :, cols] for j in range(1, 8)]
        for i in range(4):
            own = fresh if i == 0 else held[0]
            keys = jnp.concatenate([own[0, :, cols]] + common_keys, axis=0)
            values = jnp.concatenate([own[1, :, cols]] + common_values, axis=0)
            values = jnp.concatenate([values, ones], axis=1)
            scores = lax.dot_general(
                queries[i][:, cols], keys, (((1,), (1,)), ((), ())), preferred_element_type=F32
            )
            peak = jnp.max(scores, axis=-1, keepdims=True)
            weights = jnp.exp2((scores - peak) * EXP2_SCALE).astype(BF16)
            summed = jnp.dot(weights, values, preferred_element_type=F32)
            outs[i][:, cols] = summed[:, :HEAD_DIM].astype(BF16)
            parts = split3(peak) + split3(summed[:, HEAD_DIM : HEAD_DIM + 1])
            for n, part in enumerate(parts):
                marks[i] = jnp.where(lane == 6 * h + n, part.astype(F32), marks[i])
    for i in range(4):
        outs[i][:, 3 * HEAD_DIM :] = marks[i].astype(BF16)


def attend(step, queries, fresh, held, earlier=()):
    rows, width = queries[0].shape[-2:]
    out = ((rows, width + HEAD_DIM), BF16)
    return call(functools.partial(attend_kernel, step), [out] * 4, (*queries, fresh, *held, *earlier), megabytes=32)


def output_kernel(order, p0, p1, p2, p3, w, *refs):
    parts, (keep, send) = (p0, p1, p2, p3), refs[-2:]
    width = keep.shape[2]
    marks = [p[:, 3 * HEAD_DIM :].astype(F32) for p in parts]
    attended = []
    for h in range(3):
        cols = slice(h * HEAD_DIM, (h + 1) * HEAD_DIM)

        def read(mark, first):
            return mark[:, first : first + 1] + mark[:, first + 1 : first + 2] + mark[:, first + 2 : first + 3]

        peaks = [read(mark, 6 * h) for mark in marks]
        sums = [read(mark, 6 * h + 3) for mark in marks]
        peak = functools.reduce(jnp.maximum, peaks)
        factors = [jnp.exp2((one - peak) * EXP2_SCALE) for one in peaks]
        total = sum(f * s for f, s in zip(factors, sums))
        weighted = sum(f * p[:, cols].astype(F32) for f, p in zip(factors, parts))
        attended.append((weighted / total).astype(BF16))
    attended = jnp.concatenate(attended, axis=1)
    for n in range(4):
        for side, out in enumerate((keep, send)):
            cols = pl.ds(pl.multiple_of(order[2 * n + side] * width, width), width)
            out[n] = jnp.dot(attended, w[:, cols], preferred_element_type=F32).astype(BF16)


def project_out(order, partials, w_out, earlier=()):
    out = ((4, partials[0].shape[0], w_out.shape[0]), BF16)
    return call(output_kernel, [out] * 2, (order, *partials, w_out, *earlier), smem=(0,))


def on_device(hidden, stale_kv, modulation, attn_gate, w_qkv, w_out):
    width = hidden.shape[2]
    zl, core = lax.axis_index("zl"), lax.axis_index("c")
    order = jnp.stack(
        [((zl + n) % NZL) * NC + (core + s) % NC for n in range(4) for s in range(2)]
    ).astype(jnp.int32)
    w = jnp.transpose(w_qkv, (1, 0, 2))

    rows = hidden.shape[1]

    def near(pair):
        return [along_keys(pair, k) for k in (1, -1, 2)]

    quarter = ((rows, width), BF16)
    pair = ((2, rows, width), BF16)

    near_heads = [along_heads(hidden, -n) for n in (1, 2, 3)]
    stale_near = near(pass_after(stale_kv, near_heads[0]))
    own = call(
        collect_kernel,
        [((4, 2, rows, width), BF16)],
        (hidden, *near_heads, *stale_near),
        hbm=(0,),
        scratch=[pltpu.SemaphoreType.DMA],
    )[0]
    swapped = other_core(own)
    stale_copy = pass_after(stale_kv, swapped)
    opposite = other_half(stale_copy)
    queries, fresh_first, fresh_last = project(order, own, swapped, modulation, w, stale_copy)
    fresh_opposite = other_half(fresh_first)
    stale_far = near(opposite)
    queries = [queries] + [along_queries(queries, k) for k in (1, -1, 2)]
    fresh_near = near(fresh_first)

    def give_back(partials):
        return [partials[0]] + [along_queries(p, -k) for p, k in zip(partials[1:], (1, -1, 2))]

    def finish(partials, earlier_out=(), earlier_sum=()):
        keep, send = project_out(order, partials, w_out, earlier_out)
        outs = [((rows, width), F32)] + [quarter] * 3
        sums = call(sum_kernel, outs, (keep, other_core(send), *earlier_sum))
        return [sums[0]] + [along_heads(sums[n], n) for n in (1, 2, 3)]

    def update(s, parts):
        branch = parts[0]
        for part in parts[1:]:
            branch = branch + part.astype(F32)
        return (hidden[s].astype(F32) + attn_gate[s] * branch).astype(BF16)

    held = [stale_kv] + stale_near + [opposite] + stale_far
    partials_first = attend(0, queries, fresh_first, held, (fresh_opposite, *fresh_near))
    held = [fresh_first] + fresh_near + [fresh_opposite] + near(fresh_opposite)
    partials_last = attend(1, queries, fresh_last, held, partials_first[:1])
    first = finish(give_back(partials_first), partials_last[:1])
    last = finish(give_back(partials_last), first[1:])
    results = [update(0, first), update(1, last)]
    return jnp.stack(results)


def solution(mesh):
    fine = Mesh(mesh.devices.reshape(NX, NY, NZH, NZL, NC), AXES)
    patch, head = ("x", "y", "zh"), ("zl", "c")
    in_specs = (
        P(None, patch, head),
        P(None, patch, head),
        P(),
        P(None, head),
        P(None, None, head),
        P(head, None),
    )
    return jax.shard_map(
        on_device, mesh=fine, in_specs=in_specs, out_specs=P(None, patch, head), check_vma=False
    )
```

```python
import functools

import jax
import jax.numpy as jnp
from jax import lax
from jax.experimental import pallas as pl
from jax.experimental.pallas import tpu as pltpu
from jax.sharding import Mesh
from jax.sharding import PartitionSpec as P

HEAD_DIM = 128
STEPS = 2
NX, NY, NZH, NZL, NC = 4, 4, 2, 4, 2
AXES = ("x", "y", "zh", "zl", "c")
EXP2_SCALE = HEAD_DIM**-0.5 * 1.4426950408889634
F32 = jnp.float32
BF16 = jnp.bfloat16
VMEM = pl.BlockSpec(memory_space=pltpu.VMEM)
SMEM = pl.BlockSpec(memory_space=pltpu.SMEM)
HBM = pl.BlockSpec(memory_space=pltpu.HBM)
LIGHT = pl.CostEstimate(flops=1024, bytes_accessed=1024, transcendentals=0)


def device_index(x, y, zh, zl, c):
    return (((x % NX) * NY + y % NY) * NZH + zh % NZH) * NZL * NC + (zl % NZL) * NC + c % NC


def permute(array, move):
    pairs = []
    for x in range(NX):
        for y in range(NY):
            for zh in range(NZH):
                for zl in range(NZL):
                    for c in range(NC):
                        target = move(x, y, zh, zl, c)
                        pairs.append((device_index(x, y, zh, zl, c), device_index(*target)))
    return lax.ppermute(array, AXES, pairs)


def along_keys(array, k):
    return permute(array, lambda x, y, zh, zl, c: (x, y + k, zh, zl, c) if c else (x + k, y, zh, zl, c))


def along_queries(array, k):
    return permute(array, lambda x, y, zh, zl, c: (x + k, y, zh, zl, c) if c else (x, y + k, zh, zl, c))


def other_half(array):
    return permute(array, lambda x, y, zh, zl, c: (x, y, zh + 1, zl, c))


def other_core(array):
    return permute(array, lambda x, y, zh, zl, c: (x, y, zh, zl, c + 1))


def along_heads(array, k):
    return permute(array, lambda x, y, zh, zl, c: (x, y, zh, zl + k, c))


def call(body, outs, operands, hbm=(), smem=(), scratch=(), megabytes=24):
    specs = [HBM if i in hbm else SMEM if i in smem else VMEM for i in range(len(operands))]
    return pl.pallas_call(
        body,
        out_shape=[jax.ShapeDtypeStruct(shape, dtype) for shape, dtype in outs],
        in_specs=specs,
        out_specs=[VMEM] * len(outs),
        scratch_shapes=scratch,
        compiler_params=pltpu.CompilerParams(vmem_limit_bytes=megabytes * 2**20),
        cost_estimate=LIGHT,
    )(*operands)


def pass_kernel(rows, *refs):
    copy = pltpu.make_async_copy(rows, refs[-2], refs[-1])
    copy.start()
    copy.wait()


def pass_after(rows, *earlier):
    scratch = [pltpu.SemaphoreType.DMA]
    return call(pass_kernel, [(rows.shape, rows.dtype)], (rows, *earlier), hbm=(0,), scratch=scratch)[0]


def fetch_kernel(stale, hidden, mod, *refs):
    outs, sems = refs[-4:-1], refs[-1]
    for copy in load((stale, hidden, mod), outs, sems):
        copy.wait()


def collect_kernel(*refs):
    for n in range(4):
        refs[-1][n] = refs[n][...]


def normalize(step, order, pieces, mod, normed):
    pieces = [p.at[n, step] for n in range(4) for p in pieces]
    width = pieces[0].shape[1]
    total = sum(jnp.sum(p[...].astype(F32), axis=-1, keepdims=True) for p in pieces)
    mean = total / (8.0 * width)
    square = sum(
        jnp.sum(jnp.square(p[...].astype(F32) - mean), axis=-1, keepdims=True) for p in pieces
    )
    inverse = lax.rsqrt(square / (8.0 * width) + 1e-06)
    for i in range(8):
        shift_scale = mod[step, :, pl.ds(pl.multiple_of(order[i] * width, width), width)]
        value = (pieces[i][...].astype(F32) - mean) * inverse
        value = value * (1.0 + shift_scale[1:2]) + shift_scale[0:1]
        normed[:, pl.ds(pl.multiple_of(order[i] * width, width), width)] = value.astype(BF16)


def load(operands, buffers, sems):
    copies = [
        pltpu.make_async_copy(far, near, sems.at[n])
        for n, (far, near) in enumerate(zip(operands, buffers))
    ]
    for copy in copies:
        copy.start()
    return copies


def project_kernel(order, own, swapped, mod, w, *refs):
    queries, first, last, normed, w_near, sems = refs[-6:]
    parts = [(w.at[j], w_near.at[j]) for j in (1, 2, 0)]
    copies = load(*zip(*parts), sems)
    for step in range(STEPS):
        normalize(step, order, (own, swapped), mod, normed)
        for n, j in enumerate((1, 2, 0)):
            if step == 0:
                copies[n].wait()
            result = jnp.dot(normed[...], w_near[j], preferred_element_type=F32).astype(BF16)
            if j == 0:
                queries[step] = result
            else:
                (first, last)[step][j - 1] = result


def project(order, own, swapped, modulation, w, *others):
    _, _, rows, width = own.shape
    pair = ((2, rows, width), BF16)
    return call(
        project_kernel,
        [pair] * 3,
        (order, own, swapped, modulation, w, *others),
        hbm=(4,),
        smem=(0,),
        scratch=[
            pltpu.VMEM((rows, 8 * width), BF16),
            pltpu.VMEM(w.shape, BF16),
            pltpu.SemaphoreType.DMA((3,)),
        ],
        megabytes=50,
    )


def sum_kernel(keep, received, *refs):
    refs[-4][...] = keep[0].astype(F32) + received[0].astype(F32)
    for n, out in enumerate(refs[-3:]):
        out[...] = (keep[n + 1].astype(F32) + received[n + 1].astype(F32)).astype(BF16)


def split3(value):
    first = value.astype(BF16)
    rest = value - first.astype(F32)
    second = rest.astype(BF16)
    third = (rest - second.astype(F32)).astype(BF16)
    return first, second, third


def attend_kernel(step, *refs):
    queries, fresh, held, outs = refs[:4], refs[4], refs[5:13], refs[-4:]
    queries = [q.at[step] for q in queries]
    rows = queries[0].shape[0]
    lane = lax.broadcasted_iota(jnp.int32, (rows, HEAD_DIM), 1)
    marks = [jnp.zeros((rows, HEAD_DIM), F32) for _ in range(4)]
    ones = jnp.ones((8 * rows, HEAD_DIM), BF16)
    for h in range(3):
        cols = slice(h * HEAD_DIM, (h + 1) * HEAD_DIM)
        common_keys = [held[j][0, :, cols] for j in range(1, 8)]
        common_values = [held[j][1, :, cols] for j in range(1, 8)]
        for i in range(4):
            own = fresh if i == 0 else held[0]
            keys = jnp.concatenate([own[0, :, cols]] + common_keys, axis=0)
            values = jnp.concatenate([own[1, :, cols]] + common_values, axis=0)
            values = jnp.concatenate([values, ones], axis=1)
            scores = lax.dot_general(
                queries[i][:, cols], keys, (((1,), (1,)), ((), ())), preferred_element_type=F32
            )
            peak = jnp.max(scores, axis=-1, keepdims=True)
            weights = jnp.exp2((scores - peak) * EXP2_SCALE).astype(BF16)
            summed = jnp.dot(weights, values, preferred_element_type=F32)
            outs[i][:, cols] = summed[:, :HEAD_DIM].astype(BF16)
            parts = split3(peak) + split3(summed[:, HEAD_DIM : HEAD_DIM + 1])
            for n, part in enumerate(parts):
                marks[i] = jnp.where(lane == 6 * h + n, part.astype(F32), marks[i])
    for i in range(4):
        outs[i][:, 3 * HEAD_DIM :] = marks[i].astype(BF16)


def attend(step, queries, fresh, held, earlier=()):
    rows, width = queries[0].shape[-2:]
    out = ((rows, width + HEAD_DIM), BF16)
    return call(functools.partial(attend_kernel, step), [out] * 4, (*queries, fresh, *held, *earlier), megabytes=32)


def output_kernel(order, p0, p1, p2, p3, w, *refs):
    parts, (keep, send) = (p0, p1, p2, p3), refs[-2:]
    width = keep.shape[2]
    marks = [p[:, 3 * HEAD_DIM :].astype(F32) for p in parts]
    attended = []
    for h in range(3):
        cols = slice(h * HEAD_DIM, (h + 1) * HEAD_DIM)

        def read(mark, first):
            return mark[:, first : first + 1] + mark[:, first + 1 : first + 2] + mark[:, first + 2 : first + 3]

        peaks = [read(mark, 6 * h) for mark in marks]
        sums = [read(mark, 6 * h + 3) for mark in marks]
        peak = functools.reduce(jnp.maximum, peaks)
        factors = [jnp.exp2((one - peak) * EXP2_SCALE) for one in peaks]
        total = sum(f * s for f, s in zip(factors, sums))
        weighted = sum(f * p[:, cols].astype(F32) for f, p in zip(factors, parts))
        attended.append((weighted / total).astype(BF16))
    attended = jnp.concatenate(attended, axis=1)
    for n in range(4):
        for side, out in enumerate((keep, send)):
            cols = pl.ds(pl.multiple_of(order[2 * n + side] * width, width), width)
            out[n] = jnp.dot(attended, w[:, cols], preferred_element_type=F32).astype(BF16)


def project_out(order, partials, w_out, earlier=()):
    out = ((4, partials[0].shape[0], w_out.shape[0]), BF16)
    return call(output_kernel, [out] * 2, (order, *partials, w_out, *earlier), smem=(0,))


def on_device(hidden, stale_kv, modulation, attn_gate, w_qkv, w_out):
    width = hidden.shape[2]
    zl, core = lax.axis_index("zl"), lax.axis_index("c")
    order = jnp.stack(
        [((zl + n) % NZL) * NC + (core + s) % NC for n in range(4) for s in range(2)]
    ).astype(jnp.int32)
    w = jnp.transpose(w_qkv, (1, 0, 2))

    rows = hidden.shape[1]

    def near(pair):
        return [along_keys(pair, k) for k in (1, -1, 2)]

    quarter = ((rows, width), BF16)
    pair = ((2, rows, width), BF16)

    near_heads = [along_heads(hidden, -n) for n in (1, 2, 3)]
    stale_first, hidden_near, mod_near = call(
        fetch_kernel,
        [(stale_kv.shape, BF16), (hidden.shape, BF16), (modulation.shape, F32)],
        (stale_kv, hidden, modulation, near_heads[0]),
        hbm=(0, 1, 2),
        scratch=[pltpu.SemaphoreType.DMA((3,))],
    )
    stale_near = near(stale_first)
    own = call(
        collect_kernel,
        [((4, 2, rows, width), BF16)],
        (hidden_near, *near_heads, *stale_near),
    )[0]
    swapped = other_core(own)
    stale_copy = pass_after(stale_kv, swapped)
    opposite = other_half(stale_copy)
    queries, fresh_first, fresh_last = project(order, own, swapped, mod_near, w, stale_copy)
    fresh_opposite = other_half(fresh_first)
    stale_far = near(opposite)
    queries = [queries] + [along_queries(queries, k) for k in (1, -1, 2)]
    fresh_near = near(fresh_first)

    def give_back(partials):
        return [partials[0]] + [along_queries(p, -k) for p, k in zip(partials[1:], (1, -1, 2))]

    def finish(partials, earlier_out=(), earlier_sum=()):
        keep, send = project_out(order, partials, w_out, earlier_out)
        outs = [((rows, width), F32)] + [quarter] * 3
        sums = call(sum_kernel, outs, (keep, other_core(send), *earlier_sum))
        return [sums[0]] + [along_heads(sums[n], n) for n in (1, 2, 3)]

    def update(s, parts):
        branch = parts[0]
        for part in parts[1:]:
            branch = branch + part.astype(F32)
        return (hidden[s].astype(F32) + attn_gate[s] * branch).astype(BF16)

    held = [stale_kv] + stale_near + [opposite] + stale_far
    partials_first = attend(0, queries, fresh_first, held, (fresh_opposite, *fresh_near))
    held = [fresh_first] + fresh_near + [fresh_opposite] + near(fresh_opposite)
    partials_last = attend(1, queries, fresh_last, held, partials_first[:1])
    first = finish(give_back(partials_first), partials_last[:1])
    last = finish(give_back(partials_last), first[1:])
    results = [update(0, first), update(1, last)]
    return jnp.stack(results)


def solution(mesh):
    fine = Mesh(mesh.devices.reshape(NX, NY, NZH, NZL, NC), AXES)
    patch, head = ("x", "y", "zh"), ("zl", "c")
    in_specs = (
        P(None, patch, head),
        P(None, patch, head),
        P(),
        P(None, head),
        P(None, None, head),
        P(head, None),
    )
    return jax.shard_map(
        on_device, mesh=fine, in_specs=in_specs, out_specs=P(None, patch, head), check_vma=False
    )
```
